32 devices in a mesh: req: 16 (over z, y, x), tp: 2 (over core).
Axes of the slice: x: 2, y: 2, z: 4, core: 2. Of those that a mesh axis runs over, the one named last changes fastest.
Arguments:
- hidden_in: bfloat16 [512, 24, 3072], P(('req', 'tp')), may hold values from -6 to 6
- norm_gain: float32 [3072], replicated, may hold values from 0.1 to 1.9
- w_q: bfloat16 [3072, 3072], P(None, 'tp'), may hold values from -0.108253175 to 0.108253175
- w_k: bfloat16 [3072, 3072], P(None, 'tp'), may hold values from -3.35584844 to 3.35584844
- w_v: bfloat16 [3072, 3072], P(None, 'tp'), may hold values from -0.109375 to 0.109375
- w_o: bfloat16 [3072, 3072], P('tp'), may hold values from -0.109375 to 0.109375
- lengths: int32 [16, 32], P('req'), may hold values from 1 to 24, 576 in all within a row
- dest: int32 [16, 32, 1], P('req'), may hold values from 0 to 15; in each aligned block of 32 rows (0 to 31, 32 to 63, ..., all dimensions but the last counted through in order) at most 2 rows name the same one
Outputs:
- hidden_out: bfloat16 [512, 24, 3072], P(('req', 'tp'))
- cache: bfloat16 [512, 24, 2, 3072], P('req', None, None, 'tp')
The draws below stay inside these ranges and needn't reach their ends.
Inputs may be any that keep to these rules, and one draw needn't show every extreme that they name: Each replica's lengths sum to 576 and the longest is 24. `dest`: no replica names one destination for more than 2 of its requests, and some replica names one exactly 2 times.
All inputs are finite; a program needn't handle non-finite values.
Results may differ from the reference program's by a relative error of at most 0.015.
Values may be sent and summed in bfloat16 or wider, within the bound.
A program may use at most 128 MiB of HBM per device.

```python
import math
import jax
import jax.numpy as jnp
import numpy as np
from jax import lax

D = 3072
HEADS = 32
HD = 96
SLOT = 24
REQ_REP = 32
CAP = 2
HEADS_DEV = 16
REQUESTS = 512
CACHE_ROWS = 512
N_REQ = 16


def shared_base(key):
    return jnp.clip(jax.random.normal(jax.random.fold_in(key, 11), (D, HEADS * HD), jnp.float32), -6.0, 6.0)


def draw_w_q(key, part):
    return (shared_base(key) * D ** (-0.5)).astype(jnp.bfloat16)


def draw_w_k(key, part):
    noise = jnp.clip(jax.random.normal(jax.random.fold_in(key, 12), (D, HEADS * HD), jnp.float32), -6.0, 6.0)
    return (noise * D ** (-0.5)).astype(jnp.bfloat16)


def shard_levels(key, dims, pieces, smallest, high):
    level = 1.0
    for axis_at, shards_of in pieces:
        steps = jax.random.uniform(jax.random.fold_in(jax.random.fold_in(key, 6), axis_at), (shards_of,), jnp.float32, smallest / len(pieces), high / len(pieces))
        level = level * jnp.repeat(jnp.exp(steps), dims[axis_at] // shards_of).reshape((-1,) + (1,) * (len(dims) - 1 - axis_at))
    return level


def split_up(amount, total, most, slope):
    weights = [(1 << 20) // math.isqrt(rank ** slope) + 1 for rank in range(2, amount + 1)]
    spare, holding = total - most - (amount - 1), [1] * (amount - 1)
    while spare > 0:
        free = [i for i in range(amount - 1) if holding[i] < most]
        mass, left = sum([weights[i] for i in free]), spare
        for i in free:
            extra = min(most - holding[i], max(1, left * weights[i] // mass), spare)
            holding[i] = holding[i] + extra
            spare = spare - extra
    return np.array([most] + holding)


def uneven(own_key, number_of, total, reach, lean):
    if number_of == 2:
        one = jax.random.randint(own_key, (), max(1, total - reach), min(reach, total - 1) + 1)
        return jnp.stack([one, total - one])
    sizes = jnp.asarray(split_up(number_of, total, reach, lean), jnp.int32)
    pairs = (number_of - 1) // 2
    donor, taker = sizes[1:1 + 2 * pairs:2], sizes[2:2 + 2 * pairs:2]
    margin = jnp.minimum(donor - 1, reach - taker)
    shifted = jax.random.randint(jax.random.fold_in(own_key, 1), (pairs,), 0, 1 << 20) % (margin + 1)
    sizes = sizes.at[1:1 + 2 * pairs:2].set(donor - shifted).at[2:2 + 2 * pairs:2].set(taker + shifted)
    return sizes[jax.random.permutation(jax.random.fold_in(own_key, 2), number_of)]


def assign_block(own_key, own, number, rows, number_of, top, most, slope):
    sequence = jax.random.permutation(own_key, number_of)
    crowded, common = shares(number_of, rows * top, most, slope, True), shares(number_of, rows * top, most, slope, False)
    places = jnp.arange(number_of)

    def named(tallies, rotation):
        used = int((tallies > 0).sum())
        fixed = max(1, used // 4)
        moved = fixed + (places - fixed + rotation * (used - fixed)) % max(1, number_of - fixed)
        return jnp.zeros((number_of,), jnp.int32).at[sequence[jnp.where(places < fixed, places, moved)]].set(jnp.asarray(tallies, jnp.int32))

    tallies = jnp.where(number % 4 == 0, named(crowded, number // 4), named(common, number - number // 4 - 1))
    mixed = jax.random.permutation(jax.random.fold_in(own, 3), number_of)
    giver, receiver = mixed[0:number_of // 2 * 2:2], mixed[1:number_of // 2 * 2:2]
    slack = jnp.minimum(tallies[giver] - 1, most - tallies[receiver]) // 2
    slack = jnp.where((giver == sequence[0]) | (receiver == sequence[0]) | (tallies[receiver] == 0), 0, jnp.maximum(slack, 0))
    moved = jax.random.randint(jax.random.fold_in(own, 4), (number_of // 2,), 0, 1 << 20) % (slack + 1)
    tallies = tallies.at[giver].add(-moved).at[receiver].add(moved)
    items = jnp.searchsorted(jnp.cumsum(tallies), jnp.arange(rows * top), side="right").astype(jnp.int32)
    listing = items.reshape(top, rows).T
    listing = listing[jax.random.permutation(jax.random.fold_in(own, 1), rows)]
    rotation = jax.random.randint(jax.random.fold_in(own, 2), (rows, 1), 0, top)
    return jnp.take_along_axis(listing, (jnp.arange(top)[None, :] + rotation) % top, axis=1)


def shares(amount, total, bound, skew, full):
    weights = [(1 << 20) // math.isqrt(rank ** skew) + 1 for rank in range(1, amount + 1)]
    largest = bound if full else min(bound, max(-(-total // amount), total * weights[0] // sum(weights)))
    least = 1 if total - largest >= amount - 1 else 0
    given, surplus = [largest] + [least] * (amount - 1), total - largest - least * (amount - 1)
    while surplus > 0:
        candidates = [i for i in range(1, amount) if given[i] < largest] or [i for i in range(1, amount) if given[i] < bound]
        pool, remaining = sum([weights[i] for i in candidates]), surplus
        for i in candidates:
            addition = min(bound - given[i], max(1, remaining * weights[i] // pool), surplus)
            given[i] = given[i] + addition
            surplus = surplus - addition
    return np.array(given)


def bell_draw(own_key, extent, spread, bound, shards=(), kind=jnp.bfloat16):
    gain = shard_levels(own_key, extent, shards, -0.22, 0.18) if shards else 1.0
    values = jax.random.normal(own_key, extent, jnp.float32) * spread * gain
    return jnp.minimum(jnp.maximum(values, -bound), bound).astype(kind)


def setup_inputs(seed: int = 0) -> dict:
    key_list = jax.random.split(jax.random.key(seed), 9)
    hidden_in = bell_draw(key_list[0], (REQUESTS, SLOT, D), 1.0, 6.0, ((0, 32),))
    norm_gain = jnp.clip(1.0 + 0.18 * jax.random.normal(key_list[1], (D,), jnp.float32), 0.1, 1.9)
    w_q = draw_w_q(jax.random.fold_in(key_list[8], 71), 0)
    w_k = draw_w_k(jax.random.fold_in(key_list[8], 71), 0)
    w_v = bell_draw(key_list[4], (D, HEADS * HD), D ** -0.5, 0.109375, ((1, 2),))
    w_o = bell_draw(key_list[5], (HEADS * HD, D), (HEADS * HD) ** -0.5, 0.109375, ((0, 2),))
    lengths = jax.vmap(lambda own: uneven(own, REQ_REP, REQ_REP * SLOT * 3 // 4, SLOT, 2))(jax.random.split(key_list[6], N_REQ)).reshape((N_REQ, REQ_REP)).astype(jnp.int32)
    dest_keys = jax.random.split(jax.random.fold_in(key_list[7], 1), N_REQ * REQ_REP // REQ_REP)
    dest_turns = jax.random.permutation(jax.random.fold_in(key_list[7], 3), N_REQ * REQ_REP // REQ_REP)
    dest = jax.vmap(lambda own, number: assign_block(jax.random.fold_in(key_list[7], 2), own, number, REQ_REP, N_REQ, 1, CAP, 2))(dest_keys, dest_turns).reshape((N_REQ, REQ_REP, 1))
    return {"hidden_in": hidden_in, "norm_gain": norm_gain, "w_q": w_q, "w_k": w_k, "w_v": w_v, "w_o": w_o, "lengths": lengths, "dest": dest}


EPS = 1e-05

def rope_tables():
    pos = jnp.arange(SLOT, dtype=jnp.float32)
    inv = 10000.0 ** (-(jnp.arange(HD // 2, dtype=jnp.float32) * 2.0) / HD)
    angle = pos[:, None] * inv[None, :]
    cosine = jnp.concatenate([jnp.cos(angle), jnp.cos(angle)], -1)
    sine = jnp.concatenate([jnp.sin(angle), jnp.sin(angle)], -1)
    return (cosine, sine)

def rotate(x, cosine, sine):
    half = HD // 2
    turned = jnp.concatenate([-x[..., half:], x[..., :half]], -1)
    return x * cosine[None, :, None, :] + turned * sine[None, :, None, :]

def replica(x, norm_gain, w_q, w_k, w_v, w_o, lens):
    cosine, sine = rope_tables()
    xf = x.astype(jnp.float32)
    mean_sq = lax.optimization_barrier(jnp.mean(xf * xf, -1, keepdims=True))
    normed = (xf * lax.rsqrt(mean_sq + EPS) * norm_gain).astype(jnp.bfloat16)
    flat = normed.reshape(REQ_REP * SLOT, D)
    shape4 = (REQ_REP, SLOT, HEADS, HD)
    query = rotate(jnp.dot(flat, w_q, preferred_element_type=jnp.float32).reshape(shape4), cosine, sine).astype(jnp.bfloat16)
    keys = rotate(jnp.dot(flat, w_k, preferred_element_type=jnp.float32).reshape(shape4), cosine, sine).astype(jnp.bfloat16)
    values = jnp.dot(flat, w_v, preferred_element_type=jnp.float32).astype(jnp.bfloat16).reshape(shape4)
    live = jnp.arange(SLOT, dtype=jnp.int32)[None, :] < lens[:, None]
    causal = jnp.arange(SLOT)[None, :] <= jnp.arange(SLOT)[:, None]
    mask = causal[None, None, :, :] & live[:, None, None, :]
    scores = jnp.einsum('rqhd,rkhd->rhqk', query.astype(jnp.float32), keys.astype(jnp.float32)) / jnp.sqrt(jnp.float32(HD))
    scores = jnp.where(mask, scores, jnp.float32(-1e+30))
    top = lax.optimization_barrier(jnp.max(scores, -1, keepdims=True))
    expo = jnp.where(mask, jnp.exp(scores - top), 0.0)
    probs = (expo / lax.optimization_barrier(jnp.sum(expo, -1, keepdims=True))).astype(jnp.bfloat16)
    attn = jnp.einsum('rhqk,rkhd->rqhd', probs.astype(jnp.float32), values.astype(jnp.float32)).astype(jnp.bfloat16)
    attn = attn.reshape(REQ_REP * SLOT, HEADS * HD)
    group = HEADS_DEV * HD
    summed = jnp.zeros((REQ_REP * SLOT, D), jnp.float32)
    for index in range(HEADS // HEADS_DEV):
        part = jnp.dot(attn[:, index * group:(index + 1) * group], w_o[index * group:(index + 1) * group], preferred_element_type=jnp.float32).astype(jnp.bfloat16)
        part = lax.optimization_barrier(part)
        summed = summed + part.astype(jnp.float32)
    out = (summed + xf.reshape(REQ_REP * SLOT, D)).astype(jnp.bfloat16).reshape(REQ_REP, SLOT, D)
    stacked = jnp.stack([keys, values], 2)
    stacked = jnp.where(live[:, :, None, None, None], stacked, jnp.zeros_like(stacked))
    return (out, stacked.reshape(REQ_REP, SLOT, 2, HEADS * HD))

def reference(hidden_in, norm_gain, w_q, w_k, w_v, w_o, lengths, dest):
    grouped = hidden_in.reshape(N_REQ, REQ_REP, SLOT, D)

    def one(pair):
        return replica(pair[0], norm_gain, w_q, w_k, w_v, w_o, pair[1])
    outs, kvs = lax.map(one, (grouped, lengths))
    hidden_out = outs.reshape(REQUESTS, SLOT, D)
    target = dest[:, :, 0]
    same = target[:, :, None] == target[:, None, :]
    earlier = jnp.arange(REQ_REP)[None, :] < jnp.arange(REQ_REP)[:, None]
    rank = lax.optimization_barrier(jnp.sum((same & earlier[None]).astype(jnp.int32), -1)).astype(jnp.int32)
    source = jnp.arange(N_REQ, dtype=jnp.int32)[:, None]
    rows = (target * (CAP * N_REQ) + source * CAP + rank).astype(jnp.int32)
    cache = jnp.zeros((CACHE_ROWS, SLOT, 2, HEADS * HD), jnp.bfloat16)
    cache = cache.at[rows.reshape(-1)].set(kvs.reshape(REQUESTS, SLOT, 2, HEADS * HD))
    return (hidden_out, cache)
```

```python
import functools

import jax
import jax.numpy as jnp
from jax import lax
from jax.experimental import pallas as pl
from jax.experimental.pallas import tpu as pltpu
from jax.sharding import PartitionSpec as P

HD = 96
CAP = 2
EPS = 1e-05
GROUP = 384
PAIR = 2 * HD
BLOCK = 96
VMEM = 56 * 1024 * 1024


def rope_tables(slot):
    pos = jnp.arange(slot, dtype=jnp.float32)
    inv = 10000.0 ** (-(jnp.arange(HD // 2, dtype=jnp.float32) * 2.0) / HD)
    angle = pos[:, None] * inv[None, :]
    cosine, sine = jnp.cos(angle), jnp.sin(angle)
    zero = jnp.zeros_like(sine)
    heads = GROUP // HD
    cosine = jnp.tile(jnp.concatenate([cosine, cosine], -1), (1, heads))
    low = jnp.tile(jnp.concatenate([-sine, zero], -1), (1, heads))
    high = jnp.tile(jnp.concatenate([zero, sine], -1), (1, heads))
    return cosine, low, high


def rotate(x, cosine, low, high):
    rows, width = x.shape
    slot = cosine.shape[0]
    half = HD // 2
    up = pltpu.roll(x, width - half, 1)
    down = pltpu.roll(x, half, 1)
    shape = (rows // slot, slot, width)
    y = (
        x.reshape(shape) * cosine[None]
        + up.reshape(shape) * low[None]
        + down.reshape(shape) * high[None]
    )
    return y.reshape(rows, width)


def normalise(x, gain):
    xf = x.astype(jnp.float32)
    mean_sq = jnp.mean(xf * xf, -1, keepdims=True)
    return xf * lax.rsqrt(mean_sq + EPS) * gain


def attention(q, k, v, bias):
    lane = lax.broadcasted_iota(jnp.int32, (BLOCK, GROUP), 1)
    outs = []
    for pair in range(GROUP // PAIR):
        lo = 128 * pair
        cols = slice(lo, lo + 256)
        place = lane[:, cols]
        first = PAIR * pair
        own = [
            (place >= first + HD * j) & (place < first + HD * (j + 1)) for j in range(2)
        ]
        qp, kp, vp = q[:, cols], k[:, cols], v[:, cols]
        zero = jnp.zeros_like(qp)
        stacked = jnp.concatenate([jnp.where(m, qp, zero) for m in own], 0)
        s = lax.dot_general(
            stacked, kp, (((1,), (1,)), ((), ())), preferred_element_type=jnp.float32
        )
        s = s * (1.0 / HD**0.5) + jnp.concatenate([bias, bias], 0)
        e = jnp.exp(s - jnp.max(s, -1, keepdims=True))
        p = (e / jnp.sum(e, -1, keepdims=True)).astype(jnp.bfloat16)
        o = jnp.dot(p, vp, preferred_element_type=jnp.float32)
        outs.append(
            jnp.where(own[0], o[:BLOCK], jnp.where(own[1], o[BLOCK:], 0.0))
        )
    left, right = outs
    return jnp.concatenate(
        [left[:, :128], left[:, 128:] + right[:, :128], right[:, 128:]], 1
    )


def attend_kernel(
    chunk, x_ref, gain_ref, wq_ref, wk_ref, wv_ref, cos_ref, low_ref, high_ref, bias_ref,
    out_ref, normed_ref,
):
    rows = normed_ref.shape[0]

    @pl.when(pl.program_id(0) == 0)
    def _():
        def body(i, carry):
            at = pl.ds(pl.multiple_of(i * BLOCK, BLOCK), BLOCK)
            normed_ref[at, :] = normalise(x_ref[at, :], gain_ref[...]).astype(jnp.bfloat16)
            return carry

        lax.fori_loop(0, rows // BLOCK, body, 0)

    cosine, low, high = cos_ref[...], low_ref[...], high_ref[...]

    def body(i, carry):
        base = pl.multiple_of(i * chunk, chunk)
        n = normed_ref[pl.ds(base, chunk), :]
        dot = functools.partial(jnp.dot, preferred_element_type=jnp.float32)
        q = rotate(dot(n, wq_ref[...]), cosine, low, high).astype(jnp.bfloat16)
        k = rotate(dot(n, wk_ref[...]), cosine, low, high).astype(jnp.bfloat16)
        v = dot(n, wv_ref[...]).astype(jnp.bfloat16)
        for b in range(chunk // BLOCK):
            at = slice(b * BLOCK, (b + 1) * BLOCK)
            o = attention(q[at], k[at], v[at], bias_ref[i * (chunk // BLOCK) + b])
            out_ref[pl.ds(pl.multiple_of(base + b * BLOCK, BLOCK), BLOCK), :] = o.astype(
                jnp.bfloat16
            )
        return carry

    lax.fori_loop(0, rows // chunk, body, 0)


def attend(x, gain, w_q, w_k, w_v, tables, bias):
    rows, width = x.shape
    per_dev = w_q.shape[1]
    slot = tables[0].shape[0]
    whole = lambda shape: pl.BlockSpec(shape, lambda g: (0,) * len(shape))
    weight = pl.BlockSpec((width, GROUP), lambda g: (0, g))
    return pl.pallas_call(
        functools.partial(attend_kernel, 384),
        grid=(per_dev // GROUP,),
        in_specs=[
            whole((rows, width)), whole((1, width)), weight, weight, weight,
            whole((slot, GROUP)), whole((slot, GROUP)), whole((slot, GROUP)),
            whole(bias.shape),
        ],
        out_specs=pl.BlockSpec((rows, GROUP), lambda g: (0, g)),
        out_shape=jax.ShapeDtypeStruct((rows, per_dev), jnp.bfloat16),
        scratch_shapes=[pltpu.VMEM((rows, width), jnp.bfloat16)],
        compiler_params=pltpu.CompilerParams(vmem_limit_bytes=VMEM),
        cost_estimate=pl.CostEstimate(
            flops=2 * rows * width * per_dev * 3,
            bytes_accessed=2 * (rows * width + 3 * width * per_dev + rows * per_dev),
            transcendentals=0,
        ),
        name="attend",
    )(x, gain, w_q, w_k, w_v, *tables, bias)


def cache_kernel(x_ref, gain_ref, wk_ref, wv_ref, cos_ref, low_ref, high_ref, k_ref, v_ref, normed_ref):
    cap, sources, slot, width = x_ref.shape

    @pl.when(pl.program_id(0) == 0)
    def _():
        def body(i, carry):
            both = [normalise(x_ref[c, i], gain_ref[...]) for c in range(cap)]
            span = cap * slot
            at = pl.ds(pl.multiple_of(i * span, span), span)
            normed_ref[at, :] = jnp.concatenate(both, 0).astype(jnp.bfloat16)
            return carry

        lax.fori_loop(0, sources, body, 0)

    cosine, low, high = cos_ref[...], low_ref[...], high_ref[...]
    rows = normed_ref.shape[0]
    chunk = 384

    def body(i, carry):
        at = pl.ds(pl.multiple_of(i * chunk, chunk), chunk)
        n = normed_ref[at, :]
        dot = functools.partial(jnp.dot, preferred_element_type=jnp.float32)
        k_ref[at, :] = rotate(dot(n, wk_ref[...]), cosine, low, high).astype(jnp.bfloat16)
        v_ref[at, :] = dot(n, wv_ref[...]).astype(jnp.bfloat16)
        return carry

    lax.fori_loop(0, rows // chunk, body, 0)


def cache_rows(x, gain, w_k, w_v, tables):
    cap, sources, slot, width = x.shape
    rows = cap * sources * slot
    per_dev = w_k.shape[1]
    whole = lambda shape: pl.BlockSpec(shape, lambda g: (0,) * len(shape))
    single = lambda shape: pl.BlockSpec(
        shape, lambda g: (0,) * len(shape), pipeline_mode=pl.Buffered(1)
    )
    weight = pl.BlockSpec((width, GROUP), lambda g: (0, g))
    out = pl.BlockSpec((rows, GROUP), lambda g: (0, g))
    return pl.pallas_call(
        cache_kernel,
        grid=(per_dev // GROUP,),
        in_specs=[
            single(x.shape), whole((1, width)), weight, weight,
            whole((slot, GROUP)), whole((slot, GROUP)), whole((slot, GROUP)),
        ],
        out_specs=[out, out],
        out_shape=[jax.ShapeDtypeStruct((rows, per_dev), jnp.bfloat16)] * 2,
        scratch_shapes=[pltpu.VMEM((rows, width), jnp.bfloat16)],
        compiler_params=pltpu.CompilerParams(vmem_limit_bytes=VMEM),
        cost_estimate=pl.CostEstimate(
            flops=2 * rows * width * per_dev * 2,
            bytes_accessed=2 * (rows * width + 2 * width * per_dev + 2 * rows * per_dev),
            transcendentals=0,
        ),
        name="cache_rows",
    )(x, gain, w_k, w_v, *tables)


def pick_kernel(source_ref, lens_ref, x_ref, out_ref):
    slots, slot, width = out_ref.shape

    def body(i, carry):
        place = lax.broadcasted_iota(jnp.int32, (slot, width), 0)
        rows = x_ref[source_ref[i]].astype(jnp.float32)
        out_ref[i] = jnp.where(place < lens_ref[i], rows, 0.0).astype(jnp.bfloat16)
        return carry

    lax.fori_loop(0, slots, body, 0)


def pick(x, source, lens):
    _, slot, width = x.shape
    slots = source.shape[0]
    return pl.pallas_call(
        pick_kernel,
        in_specs=[
            pl.BlockSpec(memory_space=pltpu.SMEM),
            pl.BlockSpec(memory_space=pltpu.SMEM),
            pl.BlockSpec(memory_space=pltpu.VMEM),
        ],
        out_specs=pl.BlockSpec(memory_space=pltpu.VMEM),
        out_shape=jax.ShapeDtypeStruct((slots, slot, width), jnp.bfloat16),
        compiler_params=pltpu.CompilerParams(vmem_limit_bytes=VMEM),
        name="pick",
    )(source, lens, x)


def exchange(blocks, axis):
    return lax.all_to_all(blocks, axis, split_axis=0, concat_axis=0, tiled=True)


def on_device(hidden_in, norm_gain, w_q, w_k, w_v, w_o, lengths, dest):
    req_dev, slot, width = hidden_in.shape
    group = lax.axis_size("tp")
    me = lax.axis_index("tp")
    req_rep = req_dev * group
    n_req = lax.axis_size("req")
    tables = rope_tables(slot)
    gain = norm_gain[None, :]
    lens = lengths[0]

    x_all = lax.all_gather(hidden_in, "tp", axis=0, tiled=True)

    target = dest[0, :, 0]
    same = target[:, None] == target[None, :]
    earlier = jnp.arange(req_rep)[None, :] < jnp.arange(req_rep)[:, None]
    rank = jnp.sum((same & earlier).astype(jnp.int32), -1)
    wanted = jnp.arange(n_req, dtype=jnp.int32)[:, None]
    my_rank = me % CAP
    fills = (target[None, :] == wanted) & (rank[None, :] == my_rank)
    source = jnp.sum(jnp.where(fills, jnp.arange(req_rep, dtype=jnp.int32)[None, :], 0), -1)
    slot_len = jnp.sum(jnp.where(fills, lens[None, :], 0), -1)

    shares = group // CAP
    part = width // shares
    outbound = pick(x_all, source, slot_len)
    if shares > 1:
        outbound = lax.dynamic_slice_in_dim(outbound, (me // CAP) * part, part, 2)
    inbound = exchange(outbound, "req")

    live = jnp.arange(slot, dtype=jnp.int32)[None, :] < lens[:, None]
    per_block = BLOCK // slot
    token = jnp.arange(BLOCK)
    inside = (token[None, :] // slot == token[:, None] // slot) & (
        token[None, :] <= token[:, None]
    )
    bias = jnp.where(
        inside[None] & live.reshape(req_rep // per_block, 1, BLOCK), 0.0, -1e30
    ).astype(jnp.float32)
    attn = attend(x_all.reshape(req_rep * slot, width), gain, w_q, w_k, w_v, tables, bias)
    partial = jnp.dot(attn, w_o, preferred_element_type=jnp.float32).astype(jnp.bfloat16)
    partial = partial.reshape(group, req_dev, slot, width)
    mine = lax.dynamic_index_in_dim(partial, me, 0, keepdims=False).astype(jnp.float32)
    total = mine
    for step in range(1, group):
        sent = lax.dynamic_index_in_dim(partial, (me + step) % group, 0, keepdims=False)
        came = lax.ppermute(sent, "tp", [(i, (i + step) % group) for i in range(group)])
        total = total + came.astype(jnp.float32)
    hidden_out = (total + hidden_in.astype(jnp.float32)).astype(jnp.bfloat16)

    kept = lax.all_gather(inbound, "tp", axis=0, tiled=False)
    if shares > 1:
        kept = kept.reshape(shares, CAP, n_req, slot, part)
        kept = kept.transpose(1, 2, 3, 0, 4).reshape(CAP, n_req, slot, width)
    keys, values = cache_rows(kept, gain, w_k, w_v, tables)
    cache = jnp.stack([keys, values], 1).reshape(n_req * CAP, slot, 2, w_k.shape[1])
    return hidden_out, cache


def solution(mesh):
    placed = (
        P(("req", "tp"), None, None),
        P(),
        P(None, "tp"),
        P(None, "tp"),
        P(None, "tp"),
        P("tp", None),
        P("req", None),
        P("req", None, None),
    )
    return jax.shard_map(
        on_device,
        mesh=mesh,
        in_specs=placed,
        out_specs=(P(("req", "tp"), None, None), P("req", None, None, "tp")),
        check_vma=False,
    )
```

```python
import functools

import jax
import jax.numpy as jnp
from jax import lax
from jax.experimental import pallas as pl
from jax.experimental.pallas import tpu as pltpu
from jax.sharding import PartitionSpec as P

HD = 96
CAP = 2
EPS = 1e-05
GROUP = 384
PAIR = 2 * HD
BLOCK = 96
VMEM = 56 * 1024 * 1024


def rope_tables(slot):
    pos = jnp.arange(slot, dtype=jnp.float32)
    inv = 10000.0 ** (-(jnp.arange(HD // 2, dtype=jnp.float32) * 2.0) / HD)
    angle = pos[:, None] * inv[None, :]
    cosine, sine = jnp.cos(angle), jnp.sin(angle)
    zero = jnp.zeros_like(sine)
    heads = GROUP // HD
    cosine = jnp.tile(jnp.concatenate([cosine, cosine], -1), (1, heads))
    low = jnp.tile(jnp.concatenate([-sine, zero], -1), (1, heads))
    high = jnp.tile(jnp.concatenate([zero, sine], -1), (1, heads))
    return cosine, low, high


def rotate(x, cosine, low, high):
    rows, width = x.shape
    slot = cosine.shape[0]
    half = HD // 2
    up = pltpu.roll(x, width - half, 1)
    down = pltpu.roll(x, half, 1)
    shape = (rows // slot, slot, width)
    y = (
        x.reshape(shape) * cosine[None]
        + up.reshape(shape) * low[None]
        + down.reshape(shape) * high[None]
    )
    return y.reshape(rows, width)


def normalise(x, gain):
    xf = x.astype(jnp.float32)
    mean_sq = jnp.mean(xf * xf, -1, keepdims=True)
    return xf * lax.rsqrt(mean_sq + EPS) * gain


def attention(q, k, v, bias):
    lane = lax.broadcasted_iota(jnp.int32, (BLOCK, GROUP), 1)
    outs = []
    for pair in range(GROUP // PAIR):
        lo = 128 * pair
        cols = slice(lo, lo + 256)
        place = lane[:, cols]
        first = PAIR * pair
        own = [
            (place >= first + HD * j) & (place < first + HD * (j + 1)) for j in range(2)
        ]
        qp, kp, vp = q[:, cols], k[:, cols], v[:, cols]
        zero = jnp.zeros_like(qp)
        stacked = jnp.concatenate([jnp.where(m, qp, zero) for m in own], 0)
        s = lax.dot_general(
            stacked, kp, (((1,), (1,)), ((), ())), preferred_element_type=jnp.float32
        )
        s = s * (1.0 / HD**0.5) + jnp.concatenate([bias, bias], 0)
        e = jnp.exp(s - jnp.max(s, -1, keepdims=True))
        p = (e / jnp.sum(e, -1, keepdims=True)).astype(jnp.bfloat16)
        o = jnp.dot(p, vp, preferred_element_type=jnp.float32)
        outs.append(
            jnp.where(own[0], o[:BLOCK], jnp.where(own[1], o[BLOCK:], 0.0))
        )
    left, right = outs
    return jnp.concatenate(
        [left[:, :128], left[:, 128:] + right[:, :128], right[:, 128:]], 1
    )


def attend_kernel(
    chunk, x_ref, gain_ref, wq_ref, wk_ref, wv_ref, cos_ref, low_ref, high_ref, bias_ref,
    out_ref, normed_ref,
):
    rows = normed_ref.shape[0]

    @pl.when(pl.program_id(0) == 0)
    def _():
        def body(i, carry):
            at = pl.ds(pl.multiple_of(i * BLOCK, BLOCK), BLOCK)
            normed_ref[at, :] = normalise(x_ref[at, :], gain_ref[...]).astype(jnp.bfloat16)
            return carry

        lax.fori_loop(0, rows // BLOCK, body, 0)

    cosine, low, high = cos_ref[...], low_ref[...], high_ref[...]

    def body(i, carry):
        base = pl.multiple_of(i * chunk, chunk)
        n = normed_ref[pl.ds(base, chunk), :]
        dot = functools.partial(jnp.dot, preferred_element_type=jnp.float32)
        q = rotate(dot(n, wq_ref[...]), cosine, low, high).astype(jnp.bfloat16)
        k = rotate(dot(n, wk_ref[...]), cosine, low, high).astype(jnp.bfloat16)
        v = dot(n, wv_ref[...]).astype(jnp.bfloat16)
        for b in range(chunk // BLOCK):
            at = slice(b * BLOCK, (b + 1) * BLOCK)
            o = attention(q[at], k[at], v[at], bias_ref[i * (chunk // BLOCK) + b])
            out_ref[pl.ds(pl.multiple_of(base + b * BLOCK, BLOCK), BLOCK), :] = o.astype(
                jnp.bfloat16
            )
        return carry

    lax.fori_loop(0, rows // chunk, body, 0)


def attend(x, gain, w_q, w_k, w_v, tables, bias):
    rows, width = x.shape
    per_dev = w_q.shape[1]
    slot = tables[0].shape[0]
    whole = lambda shape: pl.BlockSpec(shape, lambda g: (0,) * len(shape))
    weight = pl.BlockSpec((width, GROUP), lambda g: (0, g))
    return pl.pallas_call(
        functools.partial(attend_kernel, 384),
        grid=(per_dev // GROUP,),
        in_specs=[
            whole((rows, width)), whole((1, width)), weight, weight, weight,
            whole((slot, GROUP)), whole((slot, GROUP)), whole((slot, GROUP)),
            whole(bias.shape),
        ],
        out_specs=pl.BlockSpec((rows, GROUP), lambda g: (0, g)),
        out_shape=jax.ShapeDtypeStruct((rows, per_dev), jnp.bfloat16),
        scratch_shapes=[pltpu.VMEM((rows, width), jnp.bfloat16)],
        compiler_params=pltpu.CompilerParams(vmem_limit_bytes=VMEM),
        cost_estimate=pl.CostEstimate(
            flops=2 * rows * width * per_dev * 3,
            bytes_accessed=2 * (rows * width + 3 * width * per_dev + rows * per_dev),
            transcendentals=0,
        ),
        name="attend",
    )(x, gain, w_q, w_k, w_v, *tables, bias)


def cache_kernel(x_ref, gain_ref, wk_ref, wv_ref, cos_ref, low_ref, high_ref, out_ref, normed_ref):
    cap, sources, slot, width = x_ref.shape

    @pl.when(pl.program_id(0) == 0)
    def _():
        def body(i, carry):
            both = [normalise(x_ref[c, i], gain_ref[...]) for c in range(cap)]
            span = cap * slot
            at = pl.ds(pl.multiple_of(i * span, span), span)
            normed_ref[at, :] = jnp.concatenate(both, 0).astype(jnp.bfloat16)
            return carry

        lax.fori_loop(0, sources, body, 0)

    cosine, low, high = cos_ref[...], low_ref[...], high_ref[...]
    rows = normed_ref.shape[0]
    chunk = 384

    def body(i, carry):
        at = pl.ds(pl.multiple_of(i * chunk, chunk), chunk)
        n = normed_ref[at, :]
        dot = functools.partial(jnp.dot, preferred_element_type=jnp.float32)
        keys = rotate(dot(n, wk_ref[...]), cosine, low, high)
        values = dot(n, wv_ref[...])
        out_ref[at] = jnp.stack([keys, values], 1).astype(jnp.bfloat16)
        return carry

    lax.fori_loop(0, rows // chunk, body, 0)


def cache_rows(x, gain, w_k, w_v, tables):
    cap, sources, slot, width = x.shape
    rows = cap * sources * slot
    per_dev = w_k.shape[1]
    whole = lambda shape: pl.BlockSpec(shape, lambda g: (0,) * len(shape))
    single = lambda shape: pl.BlockSpec(
        shape, lambda g: (0,) * len(shape), pipeline_mode=pl.Buffered(1)
    )
    weight = pl.BlockSpec((width, GROUP), lambda g: (0, g))
    out = pl.BlockSpec((rows, 2, GROUP), lambda g: (0, 0, g))
    return pl.pallas_call(
        cache_kernel,
        grid=(per_dev // GROUP,),
        in_specs=[
            single(x.shape), whole((1, width)), weight, weight,
            whole((slot, GROUP)), whole((slot, GROUP)), whole((slot, GROUP)),
        ],
        out_specs=out,
        out_shape=jax.ShapeDtypeStruct((rows, 2, per_dev), jnp.bfloat16),
        scratch_shapes=[pltpu.VMEM((rows, width), jnp.bfloat16)],
        compiler_params=pltpu.CompilerParams(vmem_limit_bytes=VMEM),
        cost_estimate=pl.CostEstimate(
            flops=2 * rows * width * per_dev * 2,
            bytes_accessed=2 * (rows * width + 2 * width * per_dev + 2 * rows * per_dev),
            transcendentals=0,
        ),
        name="cache_rows",
    )(x, gain, w_k, w_v, *tables)


def pick_kernel(source_ref, lens_ref, x_ref, out_ref):
    slots, slot, width = out_ref.shape

    def body(i, carry):
        place = lax.broadcasted_iota(jnp.int32, (slot, width), 0)
        rows = x_ref[source_ref[i]].astype(jnp.float32)
        out_ref[i] = jnp.where(place < lens_ref[i], rows, 0.0).astype(jnp.bfloat16)
        return carry

    lax.fori_loop(0, slots, body, 0)


def pick(x, source, lens):
    _, slot, width = x.shape
    slots = source.shape[0]
    return pl.pallas_call(
        pick_kernel,
        in_specs=[
            pl.BlockSpec(memory_space=pltpu.SMEM),
            pl.BlockSpec(memory_space=pltpu.SMEM),
            pl.BlockSpec(memory_space=pltpu.VMEM),
        ],
        out_specs=pl.BlockSpec(memory_space=pltpu.VMEM),
        out_shape=jax.ShapeDtypeStruct((slots, slot, width), jnp.bfloat16),
        compiler_params=pltpu.CompilerParams(vmem_limit_bytes=VMEM),
        name="pick",
    )(source, lens, x)


def exchange(blocks, axis):
    return lax.all_to_all(blocks, axis, split_axis=0, concat_axis=0, tiled=True)


def on_device(hidden_in, norm_gain, w_q, w_k, w_v, w_o, lengths, dest):
    req_dev, slot, width = hidden_in.shape
    group = lax.axis_size("tp")
    me = lax.axis_index("tp")
    req_rep = req_dev * group
    n_req = lax.axis_size("req")
    tables = rope_tables(slot)
    gain = norm_gain[None, :]
    lens = lengths[0]

    x_all = jnp.zeros((group, req_dev, slot, width), hidden_in.dtype)
    x_all = lax.dynamic_update_index_in_dim(x_all, hidden_in, me, 0)
    for step in range(1, group):
        came = lax.ppermute(hidden_in, "tp", [(i, (i + step) % group) for i in range(group)])
        x_all = lax.dynamic_update_index_in_dim(x_all, came, (me - step) % group, 0)
    x_all = x_all.reshape(req_rep, slot, width)

    target = dest[0, :, 0]
    same = target[:, None] == target[None, :]
    earlier = jnp.arange(req_rep)[None, :] < jnp.arange(req_rep)[:, None]
    rank = jnp.sum((same & earlier).astype(jnp.int32), -1)
    wanted = jnp.arange(n_req, dtype=jnp.int32)[:, None]
    my_rank = me % CAP
    fills = (target[None, :] == wanted) & (rank[None, :] == my_rank)
    source = jnp.sum(jnp.where(fills, jnp.arange(req_rep, dtype=jnp.int32)[None, :], 0), -1)
    slot_len = jnp.sum(jnp.where(fills, lens[None, :], 0), -1)

    shares = group // CAP
    part = width // shares
    outbound = pick(x_all, source, slot_len)
    if shares > 1:
        outbound = lax.dynamic_slice_in_dim(outbound, (me // CAP) * part, part, 2)
    inbound = exchange(outbound, "req")

    live = jnp.arange(slot, dtype=jnp.int32)[None, :] < lens[:, None]
    per_block = BLOCK // slot
    token = jnp.arange(BLOCK)
    inside = (token[None, :] // slot == token[:, None] // slot) & (
        token[None, :] <= token[:, None]
    )
    bias = jnp.where(
        inside[None] & live.reshape(req_rep // per_block, 1, BLOCK), 0.0, -1e30
    ).astype(jnp.float32)
    attn = attend(x_all.reshape(req_rep * slot, width), gain, w_q, w_k, w_v, tables, bias)
    partial = jnp.dot(attn, w_o, preferred_element_type=jnp.float32).astype(jnp.bfloat16)
    partial = partial.reshape(group, req_dev, slot, width)
    mine = lax.dynamic_index_in_dim(partial, me, 0, keepdims=False).astype(jnp.float32)
    total = mine
    for step in range(1, group):
        sent = lax.dynamic_index_in_dim(partial, (me + step) % group, 0, keepdims=False)
        came = lax.ppermute(sent, "tp", [(i, (i + step) % group) for i in range(group)])
        total = total + came.astype(jnp.float32)
    hidden_out = (total + hidden_in.astype(jnp.float32)).astype(jnp.bfloat16)

    kept = lax.all_gather(inbound, "tp", axis=0, tiled=False)
    if shares > 1:
        kept = kept.reshape(shares, CAP, n_req, slot, part)
        kept = kept.transpose(1, 2, 3, 0, 4).reshape(CAP, n_req, slot, width)
    cache = cache_rows(kept, gain, w_k, w_v, tables)
    cache = cache.reshape(n_req * CAP, slot, 2, w_k.shape[1])
    return hidden_out, cache


def solution(mesh):
    placed = (
        P(("req", "tp"), None, None),
        P(),
        P(None, "tp"),
        P(None, "tp"),
        P(None, "tp"),
        P("tp", None),
        P("req", None),
        P("req", None, None),
    )
    return jax.shard_map(
        on_device,
        mesh=mesh,
        in_specs=placed,
        out_specs=(P(("req", "tp"), None, None), P("req", None, None, "tp")),
        check_vma=False,
    )
```

```python
import functools

import jax
import jax.numpy as jnp
from jax import lax
from jax.experimental import pallas as pl
from jax.experimental.pallas import tpu as pltpu
from jax.sharding import PartitionSpec as P

HD = 96
CAP = 2
EPS = 1e-05
GROUP = 384
PAIR = 2 * HD
BLOCK = 96
VMEM = 58 * 1024 * 1024


def rope_tables(slot):
    pos = jnp.arange(slot, dtype=jnp.float32)
    inv = 10000.0 ** (-(jnp.arange(HD // 2, dtype=jnp.float32) * 2.0) / HD)
    angle = pos[:, None] * inv[None, :]
    cosine, sine = jnp.cos(angle), jnp.sin(angle)
    zero = jnp.zeros_like(sine)
    heads = GROUP // HD
    cosine = jnp.tile(jnp.concatenate([cosine, cosine], -1), (1, heads))
    low = jnp.tile(jnp.concatenate([-sine, zero], -1), (1, heads))
    high = jnp.tile(jnp.concatenate([zero, sine], -1), (1, heads))
    return cosine, low, high


def rotate(x, cosine, low, high):
    rows, width = x.shape
    slot = cosine.shape[0]
    half = HD // 2
    up = pltpu.roll(x, width - half, 1)
    down = pltpu.roll(x, half, 1)
    shape = (rows // slot, slot, width)
    y = (
        x.reshape(shape) * cosine[None]
        + up.reshape(shape) * low[None]
        + down.reshape(shape) * high[None]
    )
    return y.reshape(rows, width)


def normalise(x, gain):
    xf = x.astype(jnp.float32)
    mean_sq = jnp.mean(xf * xf, -1, keepdims=True)
    return xf * lax.rsqrt(mean_sq + EPS) * gain


def attention(q, k, v, bias):
    lane = lax.broadcasted_iota(jnp.int32, (BLOCK, GROUP), 1)
    outs = []
    for pair in range(GROUP // PAIR):
        lo = 128 * pair
        cols = slice(lo, lo + 256)
        place = lane[:, cols]
        first = PAIR * pair
        own = [
            (place >= first + HD * j) & (place < first + HD * (j + 1)) for j in range(2)
        ]
        qp, kp, vp = q[:, cols], k[:, cols], v[:, cols]
        zero = jnp.zeros_like(qp)
        stacked = jnp.concatenate([jnp.where(m, qp, zero) for m in own], 0)
        s = lax.dot_general(
            stacked, kp, (((1,), (1,)), ((), ())), preferred_element_type=jnp.float32
        )
        s = s * (1.0 / HD**0.5) + jnp.concatenate([bias, bias], 0)
        e = jnp.exp(s - jnp.max(s, -1, keepdims=True))
        p = (e / jnp.sum(e, -1, keepdims=True)).astype(jnp.bfloat16)
        o = jnp.dot(p, vp, preferred_element_type=jnp.float32)
        outs.append(
            jnp.where(own[0], o[:BLOCK], jnp.where(own[1], o[BLOCK:], 0.0))
        )
    left, right = outs
    return jnp.concatenate(
        [left[:, :128], left[:, 128:] + right[:, :128], right[:, 128:]], 1
    )


def attend_kernel(
    chunk, x_ref, gain_ref, wq_ref, wk_ref, wv_ref, cos_ref, low_ref, high_ref, bias_ref,
    out_ref, normed_ref,
):
    rows = normed_ref.shape[0]

    @pl.when(pl.program_id(0) == 0)
    def _():
        def body(i, carry):
            at = pl.ds(pl.multiple_of(i * BLOCK, BLOCK), BLOCK)
            normed_ref[at, :] = normalise(x_ref[at, :], gain_ref[...]).astype(jnp.bfloat16)
            return carry

        lax.fori_loop(0, rows // BLOCK, body, 0)

    cosine, low, high = cos_ref[...], low_ref[...], high_ref[...]

    def body(i, carry):
        base = pl.multiple_of(i * chunk, chunk)
        n = normed_ref[pl.ds(base, chunk), :]
        dot = functools.partial(jnp.dot, preferred_element_type=jnp.float32)
        q = rotate(dot(n, wq_ref[...]), cosine, low, high).astype(jnp.bfloat16)
        k = rotate(dot(n, wk_ref[...]), cosine, low, high).astype(jnp.bfloat16)
        v = dot(n, wv_ref[...]).astype(jnp.bfloat16)
        for b in range(chunk // BLOCK):
            at = slice(b * BLOCK, (b + 1) * BLOCK)
            to = pl.ds(pl.multiple_of(base + b * BLOCK, BLOCK), BLOCK)
            seen = bias_ref[i * (chunk // BLOCK) + b]
            for first in range(0, q.shape[1], GROUP):
                heads = slice(first, first + GROUP)
                o = attention(q[at, heads], k[at, heads], v[at, heads], seen)
                out_ref[to, heads] = o.astype(jnp.bfloat16)
        return carry

    lax.fori_loop(0, rows // chunk, body, 0)


def attend(x, gain, w_q, w_k, w_v, tables, bias):
    rows, width = x.shape
    per_dev = w_q.shape[1]
    slot = tables[0].shape[0]
    whole = lambda shape: pl.BlockSpec(shape, lambda g: (0,) * len(shape))
    cols = min(2 * GROUP, per_dev)
    tables = [jnp.tile(t, (1, cols // GROUP)) for t in tables]
    weight = pl.BlockSpec((width, cols), lambda g: (0, g))
    return pl.pallas_call(
        functools.partial(attend_kernel, 384),
        grid=(per_dev // cols,),
        in_specs=[
            pl.BlockSpec((rows, width), lambda g: (0, 0), pipeline_mode=pl.Buffered(1)),
            whole((1, width)), weight, weight, weight,
            whole((slot, cols)), whole((slot, cols)), whole((slot, cols)),
            whole(bias.shape),
        ],
        out_specs=pl.BlockSpec((rows, cols), lambda g: (0, g)),
        out_shape=jax.ShapeDtypeStruct((rows, per_dev), jnp.bfloat16),
        scratch_shapes=[pltpu.VMEM((rows, width), jnp.bfloat16)],
        compiler_params=pltpu.CompilerParams(vmem_limit_bytes=VMEM),
        cost_estimate=pl.CostEstimate(
            flops=2 * rows * width * per_dev * 3,
            bytes_accessed=2 * (rows * width + 3 * width * per_dev + rows * per_dev),
            transcendentals=0,
        ),
        name="attend",
    )(x, gain, w_q, w_k, w_v, *tables, bias)


def cache_kernel(x_ref, gain_ref, wk_ref, wv_ref, cos_ref, low_ref, high_ref, out_ref, normed_ref):
    cap, sources, slot, width = x_ref.shape

    @pl.when(pl.program_id(0) == 0)
    def _():
        def body(i, carry):
            both = [normalise(x_ref[c, i], gain_ref[...]) for c in range(cap)]
            span = cap * slot
            at = pl.ds(pl.multiple_of(i * span, span), span)
            normed_ref[at, :] = jnp.concatenate(both, 0).astype(jnp.bfloat16)
            return carry

        lax.fori_loop(0, sources, body, 0)

    cosine, low, high = cos_ref[...], low_ref[...], high_ref[...]
    rows = normed_ref.shape[0]
    chunk = 384

    def body(i, carry):
        at = pl.ds(pl.multiple_of(i * chunk, chunk), chunk)
        n = normed_ref[at, :]
        dot = functools.partial(jnp.dot, preferred_element_type=jnp.float32)
        keys = rotate(dot(n, wk_ref[...]), cosine, low, high)
        values = dot(n, wv_ref[...])
        out_ref[at] = jnp.stack([keys, values], 1).astype(jnp.bfloat16)
        return carry

    lax.fori_loop(0, rows // chunk, body, 0)


def cache_rows(x, gain, w_k, w_v, tables):
    cap, sources, slot, width = x.shape
    rows = cap * sources * slot
    per_dev = w_k.shape[1]
    whole = lambda shape: pl.BlockSpec(shape, lambda g: (0,) * len(shape))
    single = lambda shape: pl.BlockSpec(
        shape, lambda g: (0,) * len(shape), pipeline_mode=pl.Buffered(1)
    )
    cols = min(2 * GROUP, per_dev)
    tables = [jnp.tile(t, (1, cols // GROUP)) for t in tables]
    weight = pl.BlockSpec((width, cols), lambda g: (0, g))
    out = pl.BlockSpec((rows, 2, cols), lambda g: (0, 0, g))
    return pl.pallas_call(
        cache_kernel,
        grid=(per_dev // cols,),
        in_specs=[
            single(x.shape), whole((1, width)), weight, weight,
            whole((slot, cols)), whole((slot, cols)), whole((slot, cols)),
        ],
        out_specs=out,
        out_shape=jax.ShapeDtypeStruct((rows, 2, per_dev), jnp.bfloat16),
        scratch_shapes=[pltpu.VMEM((rows, width), jnp.bfloat16)],
        compiler_params=pltpu.CompilerParams(vmem_limit_bytes=VMEM),
        cost_estimate=pl.CostEstimate(
            flops=2 * rows * width * per_dev * 2,
            bytes_accessed=2 * (rows * width + 2 * width * per_dev + 2 * rows * per_dev),
            transcendentals=0,
        ),
        name="cache_rows",
    )(x, gain, w_k, w_v, *tables)


def pick_kernel(source_ref, lens_ref, x_ref, out_ref):
    slots, slot, width = out_ref.shape

    def body(i, carry):
        place = lax.broadcasted_iota(jnp.int32, (slot, width), 0)
        rows = x_ref[source_ref[i]].astype(jnp.float32)
        out_ref[i] = jnp.where(place < lens_ref[i], rows, 0.0).astype(jnp.bfloat16)
        return carry

    lax.fori_loop(0, slots, body, 0)


def pick(x, source, lens):
    _, slot, width = x.shape
    slots = source.shape[0]
    return pl.pallas_call(
        pick_kernel,
        in_specs=[
            pl.BlockSpec(memory_space=pltpu.SMEM),
            pl.BlockSpec(memory_space=pltpu.SMEM),
            pl.BlockSpec(memory_space=pltpu.VMEM),
        ],
        out_specs=pl.BlockSpec(memory_space=pltpu.VMEM),
        out_shape=jax.ShapeDtypeStruct((slots, slot, width), jnp.bfloat16),
        compiler_params=pltpu.CompilerParams(vmem_limit_bytes=VMEM),
        name="pick",
    )(source, lens, x)


def exchange(blocks, axis):
    return lax.all_to_all(blocks, axis, split_axis=0, concat_axis=0, tiled=True)


def on_device(hidden_in, norm_gain, w_q, w_k, w_v, w_o, lengths, dest):
    req_dev, slot, width = hidden_in.shape
    group = lax.axis_size("tp")
    me = lax.axis_index("tp")
    req_rep = req_dev * group
    n_req = lax.axis_size("req")
    tables = rope_tables(slot)
    gain = norm_gain[None, :]
    lens = lengths[0]

    x_all = jnp.zeros((group, req_dev, slot, width), hidden_in.dtype)
    x_all = lax.dynamic_update_index_in_dim(x_all, hidden_in, me, 0)
    for step in range(1, group):
        came = lax.ppermute(hidden_in, "tp", [(i, (i + step) % group) for i in range(group)])
        x_all = lax.dynamic_update_index_in_dim(x_all, came, (me - step) % group, 0)
    x_all = x_all.reshape(req_rep, slot, width)

    target = dest[0, :, 0]
    same = target[:, None] == target[None, :]
    earlier = jnp.arange(req_rep)[None, :] < jnp.arange(req_rep)[:, None]
    rank = jnp.sum((same & earlier).astype(jnp.int32), -1)
    wanted = jnp.arange(n_req, dtype=jnp.int32)[:, None]
    my_rank = me % CAP
    fills = (target[None, :] == wanted) & (rank[None, :] == my_rank)
    source = jnp.sum(jnp.where(fills, jnp.arange(req_rep, dtype=jnp.int32)[None, :], 0), -1)
    slot_len = jnp.sum(jnp.where(fills, lens[None, :], 0), -1)

    shares = group // CAP
    part = width // shares
    outbound = pick(x_all, source, slot_len)
    if shares > 1:
        outbound = lax.dynamic_slice_in_dim(outbound, (me // CAP) * part, part, 2)
    inbound = exchange(outbound, "req")

    live = jnp.arange(slot, dtype=jnp.int32)[None, :] < lens[:, None]
    per_block = BLOCK // slot
    token = jnp.arange(BLOCK)
    inside = (token[None, :] // slot == token[:, None] // slot) & (
        token[None, :] <= token[:, None]
    )
    bias = jnp.where(
        inside[None] & live.reshape(req_rep // per_block, 1, BLOCK), 0.0, -1e30
    ).astype(jnp.float32)
    attn = attend(x_all.reshape(req_rep * slot, width), gain, w_q, w_k, w_v, tables, bias)
    partial = jnp.dot(attn, w_o, preferred_element_type=jnp.float32).astype(jnp.bfloat16)
    partial = partial.reshape(group, req_dev, slot, width)
    mine = lax.dynamic_index_in_dim(partial, me, 0, keepdims=False).astype(jnp.float32)
    total = mine
    for step in range(1, group):
        sent = lax.dynamic_index_in_dim(partial, (me + step) % group, 0, keepdims=False)
        came = lax.ppermute(sent, "tp", [(i, (i + step) % group) for i in range(group)])
        total = total + came.astype(jnp.float32)
    hidden_out = (total + hidden_in.astype(jnp.float32)).astype(jnp.bfloat16)

    kept = lax.all_gather(inbound, "tp", axis=0, tiled=False)
    if shares > 1:
        kept = kept.reshape(shares, CAP, n_req, slot, part)
        kept = kept.transpose(1, 2, 3, 0, 4).reshape(CAP, n_req, slot, width)
    cache = cache_rows(kept, gain, w_k, w_v, tables)
    cache = cache.reshape(n_req * CAP, slot, 2, w_k.shape[1])
    return hidden_out, cache


def solution(mesh):
    placed = (
        P(("req", "tp"), None, None),
        P(),
        P(None, "tp"),
        P(None, "tp"),
        P(None, "tp"),
        P("tp", None),
        P("req", None),
        P("req", None, None),
    )
    return jax.shard_map(
        on_device,
        mesh=mesh,
        in_specs=placed,
        out_specs=(P(("req", "tp"), None, None), P("req", None, None, "tp")),
        check_vma=False,
    )
```
